32 devices in a mesh: lat: 16 (over z, y, core), lon: 2 (over x).
Axes of the slice: x: 2, y: 2, z: 4, core: 2. Of those that a mesh axis runs over, the one named last changes fastest.
Arguments:
- source_field: bfloat16 [384, 768, 384], P('lat', 'lon'), may hold values from -6 to 6
- cotangent: bfloat16 [384, 768, 384], P('lat', 'lon'), may hold values from -6 to 6
- weight: bfloat16 [3, 384, 384], replicated, may hold values from -0.1875 to 0.1875
- spectral_gain: float32 [384, 384], replicated, may hold values from 0.1 to 1.9
- legendre: bfloat16 [384, 384, 384], P(('lat', 'lon')), may hold values from -0.3125 to 0.3125
- support_lat: int32 [384, 16], replicated, may hold values from -2 to 2
- support_lon: int32 [384, 16], replicated, may hold values from -4 to 4
- support_val: float32 [384, 16, 3], replicated, may hold values from -1.5 to 1.5
- order_map: int32 [384], replicated, may hold values from 0 to 383, each once
Outputs:
- result: bfloat16 [384, 768, 384], P('lat', 'lon')
- grad_input: bfloat16 [384, 768, 384], P('lat', 'lon')
- grad_weight: float32 [3, 384, 384], replicated
- grad_gain: float32 [384, 384], replicated
The draws below stay inside these ranges and needn't reach their ends.
Inputs may be any that keep to these rules, and one draw needn't show every extreme that they name: `order_map`: each order appears once.
All inputs are finite; a program needn't handle non-finite values.
Results may differ from the reference program's by a relative error of at most 0.009.
Values may be sent and summed in bfloat16 or wider, within the bound.
A program may use at most 512 MiB of HBM per device.

```python
import math
import jax
import jax.numpy as jnp
from jax import lax

C = 384
NLON = 768
M = 384
L = 384
K = 3
H = 2
DW = 4
S = 16
LAT_DEV = 24
NLAT = 384
N_LAT = 16


def set_ends(drawn, stream_key, smallest, high):
    index_at = [jax.random.randint(jax.random.fold_in(stream_key, axis), (), 0, length) for axis, length in enumerate(drawn.shape)]
    main_axis = drawn.shape.index(max(drawn.shape))
    beside = index_at[:main_axis] + [(index_at[main_axis] + 1) % drawn.shape[main_axis]] + index_at[main_axis + 1:]
    return drawn.at[tuple(index_at)].set(smallest).at[tuple(beside)].set(high)


def shard_levels(rng, extent, shards, low, top_value):
    def one(position, shards_of):
        steps = jax.random.uniform(jax.random.fold_in(jax.random.fold_in(rng, 6), position), (shards_of,), jnp.float32, low / len(shards), top_value / len(shards))
        return jnp.repeat(jnp.exp(steps), extent[position] // shards_of).reshape((-1,) + (1,) * (len(extent) - position - 1))

    factor_of = one(*shards[0])
    for cut in shards[1:]:
        factor_of = factor_of * one(*cut)
    return factor_of


def gaussian(key, dims, spread, limit, shards=(), kind=jnp.bfloat16):
    array = jax.random.normal(key, dims, jnp.float32) * spread
    if len(shards) > 0:
        array = shard_levels(key, dims, shards, -0.22, 0.18) * array
    return jnp.clip(array, min=-limit, max=limit).astype(kind)


def setup_inputs(seed: int = 0) -> dict:
    splits = jax.random.split(jax.random.key(seed), 10)
    return {
        "source_field": gaussian(splits[0], (NLAT, NLON, C), 1.0, 6.0, ((0, 16), (1, 2))),
        "cotangent": gaussian(splits[1], (NLAT, NLON, C), 1.0, 6.0, ((0, 16), (1, 2))),
        "weight": gaussian(splits[2], (K, C, C), (K * C) ** -0.5, 0.1875),
        "spectral_gain": jnp.clip(1.0 + 0.18 * jax.random.normal(splits[3], (L, C), jnp.float32), 0.1, 1.9),
        "legendre": gaussian(splits[4], (M, L, NLAT), NLAT ** -0.5, 0.3125, ((0, 32),)),
        "support_lat": set_ends(jax.random.randint(splits[5], (NLAT, S), 0 - H, H + 1), jax.random.fold_in(splits[5], 1), 0 - H, H).astype(jnp.int32),
        "support_lon": set_ends(jax.random.randint(splits[6], (NLAT, S), 0 - DW, DW + 1), jax.random.fold_in(splits[6], 1), 0 - DW, DW).astype(jnp.int32),
        "support_val": gaussian(splits[7], (NLAT, S, K), S ** -0.5, 1.5, (), jnp.float32),
        "order_map": jax.random.permutation(splits[8], M).astype(jnp.int32),
    }


SQRT_HALF = 0.7071067811865476
INV_SQRT_TAU = 0.3989422804014327

def gelu_value(values):
    return 0.5 * values * (1.0 + lax.erf(values * SQRT_HALF))

def gelu_slope(values):
    return 0.5 * (1.0 + lax.erf(values * SQRT_HALF)) + values * INV_SQRT_TAU * jnp.exp(-0.5 * values * values)

def tap_table(support_lat, support_lon, support_val):
    lat_steps = jnp.arange(2 * H + 1, dtype=jnp.int32) - H
    lon_steps = jnp.arange(2 * DW + 1, dtype=jnp.int32) - DW
    lat_onehot = (support_lat[:, :, None] == lat_steps[None, None, :]).astype(jnp.float32)
    lon_onehot = (support_lon[:, :, None] == lon_steps[None, None, :]).astype(jnp.float32)
    return jnp.einsum('tsk,tsa,tsd->tkad', support_val.astype(jnp.float32), lat_onehot, lon_onehot, precision=lax.Precision.HIGHEST)

def dft_table(order_map):
    frequency = jnp.repeat(order_map.astype(jnp.int32), 2)
    component = jnp.arange(frequency.shape[0], dtype=jnp.int32) % 2
    longitude = jnp.arange(NLON, dtype=jnp.int32)
    cycles = longitude[:, None] * frequency[None, :] % NLON
    angles = cycles.astype(jnp.float32) * (2.0 * math.pi / NLON)
    matrix = jnp.where(component[None, :] == 0, jnp.cos(angles), -jnp.sin(angles)) * math.sqrt(2.0 / NLON)
    return matrix.astype(jnp.bfloat16)

def apply_taps(padded, tap_rows, row_count, col_count, mirror):
    summed = jnp.zeros((row_count, col_count, K, padded.shape[2]), jnp.float32)
    for lat_tap in range(2 * H + 1):
        for lon_tap in range(2 * DW + 1):
            if mirror:
                row_start = 2 * H - lat_tap
                col_start = 2 * DW - lon_tap
                tap_coef = tap_rows[row_start:row_start + row_count, :, lat_tap, lon_tap]
            else:
                row_start = lat_tap
                col_start = lon_tap
                tap_coef = tap_rows[H:H + row_count, :, lat_tap, lon_tap]
            window = padded[row_start:row_start + row_count, col_start:col_start + col_count, :].astype(jnp.float32)
            summed = summed + tap_coef[:, None, :, None] * window[:, :, None, :]
    return summed.astype(jnp.bfloat16)

def wrap_pad(field):
    lon_padded = jnp.concatenate([field[:, NLON - DW:], field, field[:, :DW]], axis=1)
    return jnp.pad(lon_padded, ((H, H), (0, 0), (0, 0)))

def reference(source_field, cotangent, weight, spectral_gain, legendre, support_lat, support_lon, support_val, order_map):
    lat_total = LAT_DEV * N_LAT
    tap_weights = tap_table(support_lat, support_lon, support_val)
    tap_pad = jnp.pad(tap_weights, ((H, H), (0, 0), (0, 0), (0, 0)))
    dft_matrix = dft_table(order_map).astype(jnp.float32)
    quad_weights = jnp.sin(math.pi * (jnp.arange(lat_total, dtype=jnp.int32).astype(jnp.float32) + 0.5) / lat_total)
    flat_weight = weight.reshape(K * C, C)
    source_pad = wrap_pad(source_field)
    block_ids = jnp.arange(N_LAT, dtype=jnp.int32)

    def band_taps(block_number):
        offset = block_number * LAT_DEV
        window = lax.dynamic_slice_in_dim(source_pad, offset, LAT_DEV + 2 * H, 0)
        tap_rows = lax.dynamic_slice_in_dim(tap_pad, offset, LAT_DEV + 2 * H, 0)
        return apply_taps(window, tap_rows, LAT_DEV, NLON, False).reshape(LAT_DEV * NLON, K * C)

    def forward_band(block_number):
        offset = block_number * LAT_DEV
        conv_out = jnp.dot(band_taps(block_number), flat_weight, preferred_element_type=jnp.float32).astype(jnp.bfloat16)
        hidden = gelu_value(conv_out.astype(jnp.float32)).astype(jnp.bfloat16).reshape(LAT_DEV, NLON, C)
        band_quad = lax.dynamic_slice_in_dim(quad_weights, offset, LAT_DEV, 0)
        spectral = jnp.einsum('tpc,pj->tjc', hidden.astype(jnp.float32), dft_matrix) * band_quad[:, None, None]
        return (conv_out.reshape(LAT_DEV, NLON, C), spectral.astype(jnp.bfloat16))
    conv_out, spectral = lax.map(forward_band, block_ids)
    conv_out = conv_out.reshape(lat_total, NLON, C)
    spectral = spectral.reshape(lat_total, M, 2, C)
    table_wide = legendre.astype(jnp.float32)
    coefficients = jnp.einsum('olt,toqc->olqc', table_wide, spectral.astype(jnp.float32))
    filtered = (spectral_gain[None, :, None, :] * coefficients).astype(jnp.bfloat16)
    synthesized = jnp.einsum('olt,olqc->toqc', table_wide, filtered.astype(jnp.float32)).astype(jnp.bfloat16)
    synthesized = synthesized.reshape(N_LAT, LAT_DEV, 2 * M, C)
    conv_bands = conv_out.reshape(N_LAT, LAT_DEV, NLON, C)

    def output_band(pair):
        synth_band, conv_band = pair
        branch = jnp.einsum('tjc,pj->tpc', synth_band.astype(jnp.float32), dft_matrix).astype(jnp.bfloat16)
        return (conv_band.astype(jnp.float32) + branch.astype(jnp.float32)).astype(jnp.bfloat16)
    result = lax.map(output_band, (synthesized, conv_bands)).reshape(lat_total, NLON, C)

    def cot_band(cot_rows):
        return jnp.einsum('tpc,pj->tjc', cot_rows.astype(jnp.float32), dft_matrix).astype(jnp.bfloat16)
    cot_spectral = lax.map(cot_band, cotangent.reshape(N_LAT, LAT_DEV, NLON, C)).reshape(lat_total, M, 2, C)
    cot_coefficients = jnp.einsum('olt,toqc->olqc', table_wide, cot_spectral.astype(jnp.float32))
    grad_gain = lax.optimization_barrier(jnp.sum(coefficients * cot_coefficients, axis=(0, 2))) / math.sqrt(2.0 * M)
    cot_filtered = (spectral_gain[None, :, None, :] * cot_coefficients).astype(jnp.bfloat16)
    cot_synth = jnp.einsum('olt,olqc->toqc', table_wide, cot_filtered.astype(jnp.float32))
    cot_synth = (cot_synth * quad_weights[:, None, None, None]).astype(jnp.bfloat16)
    cot_synth = cot_synth.reshape(N_LAT, LAT_DEV, 2 * M, C)

    def cot_conv_band(triple):
        synth_band, conv_band, cot_rows = triple
        cot_hidden = jnp.einsum('tjc,pj->tpc', synth_band.astype(jnp.float32), dft_matrix).astype(jnp.bfloat16)
        slope = gelu_slope(conv_band.astype(jnp.float32))
        return (cot_rows.astype(jnp.float32) + cot_hidden.astype(jnp.float32) * slope).astype(jnp.bfloat16)
    cot_conv = lax.map(cot_conv_band, (cot_synth, conv_bands, cotangent.reshape(N_LAT, LAT_DEV, NLON, C)))
    cot_conv = cot_conv.reshape(lat_total, NLON, C)
    cot_pad = wrap_pad(cot_conv)

    def grad_band(summed, block_number):
        offset = block_number * LAT_DEV
        taps_flat = band_taps(block_number)
        cot_rows = lax.dynamic_slice_in_dim(cot_conv, offset, LAT_DEV, 0).reshape(LAT_DEV * NLON, C)
        partial_sum = jnp.dot(taps_flat.T, cot_rows, preferred_element_type=jnp.float32)
        window = lax.dynamic_slice_in_dim(cot_pad, offset, LAT_DEV + 2 * H, 0)
        tap_rows = lax.dynamic_slice_in_dim(tap_pad, offset, LAT_DEV + 2 * H, 0)
        back_taps = apply_taps(window, tap_rows, LAT_DEV, NLON, True).reshape(LAT_DEV * NLON, K, C)
        grad_rows = jnp.einsum('nkf,kcf->nc', back_taps.astype(jnp.float32), weight.astype(jnp.float32))
        return (summed + partial_sum, grad_rows.astype(jnp.bfloat16))
    summed, grad_input = lax.scan(grad_band, jnp.zeros((K * C, C), jnp.float32), block_ids)
    grad_input = grad_input.reshape(lat_total, NLON, C)
    grad_weight = (summed / math.sqrt(1.0 * lat_total * NLON)).reshape(K, C, C)
    return (result, grad_input, grad_weight, grad_gain)
```

```python
import functools
import math

import jax
import jax.numpy as jnp
from jax import lax
from jax.experimental import pallas as pl
from jax.experimental.pallas import tpu as pltpu
from jax.sharding import PartitionSpec as P

NLON = 768
M = 384
K = 3
H = 2
DW = 4


SQRT_HALF = 0.7071067811865476
INV_SQRT_TAU = 0.3989422804014327


def gelu_value(values):
    return 0.5 * values * (1.0 + lax.erf(values * SQRT_HALF))


def gelu_slope(values):
    return 0.5 * (1.0 + lax.erf(values * SQRT_HALF)) + values * INV_SQRT_TAU * jnp.exp(
        -0.5 * values * values
    )


def tap_table(support_lat, support_lon, support_val):
    lat_steps = jnp.arange(2 * H + 1, dtype=jnp.int32) - H
    lon_steps = jnp.arange(2 * DW + 1, dtype=jnp.int32) - DW
    lat_onehot = (support_lat[:, :, None] == lat_steps[None, None, :]).astype(jnp.float32)
    lon_onehot = (support_lon[:, :, None] == lon_steps[None, None, :]).astype(jnp.float32)
    return jnp.einsum(
        "tsk,tsa,tsd->tkad", support_val, lat_onehot, lon_onehot, precision=lax.Precision.HIGHEST
    )


def dft_table(longitude, frequency):
    cycles = longitude[:, None] * frequency[None, :] % NLON
    angles = cycles.astype(jnp.float32) * (2.0 * math.pi / NLON)
    matrix = jnp.concatenate([jnp.cos(angles), -jnp.sin(angles)], axis=1) * math.sqrt(2.0 / NLON)
    return matrix.astype(jnp.bfloat16)


P_BLOCK = 96
Q_BLOCK = 128
N_LAT_TAPS = 2 * H + 1
VMEM_LIMIT = 48 * 1024 * 1024
GROUP = 8
LANES = 128


def lane_tiles(wide):
    return [(start, min(LANES, wide - start)) for start in range(0, wide, LANES)]


def wide_scratch(rows, wide):
    return pltpu.VMEM((len(lane_tiles(wide)), rows, LANES), jnp.float32)


def cost(micros):
    return pl.CostEstimate(
        flops=int(micros * 3.3e8), bytes_accessed=int(micros * 1e6), transcendentals=0
    )


def tap_coefficients(tap_rows, row_count, mirror):
    coef_list = []
    for place in range(N_LAT_TAPS):
        if mirror:
            taken = tap_rows[place : place + row_count, :, N_LAT_TAPS - 1 - place, ::-1]
        else:
            taken = tap_rows[H : H + row_count, :, place, :]
        coef_list.append(taken)
    coefs = jnp.stack(coef_list, axis=2).reshape(row_count, K * N_LAT_TAPS, 2 * DW + 1)
    return jnp.pad(coefs, ((0, 0), (0, 1), (0, Q_BLOCK - 2 * DW - 1)))


def fill_taps(coef_ref, window_refs, band_ref, taps_ref):
    for k in range(K):
        for place in range(N_LAT_TAPS):
            index = k * N_LAT_TAPS + place
            row = jnp.broadcast_to(coef_ref[0, index : index + 1, :], (P_BLOCK, Q_BLOCK))
            band = pltpu.roll(row, 0, 1, stride=1, stride_axis=0)
            band_ref[
                k * P_BLOCK : (k + 1) * P_BLOCK, place * Q_BLOCK : (place + 1) * Q_BLOCK
            ] = band.astype(jnp.bfloat16)
    col_count, wide = taps_ref.shape
    chan_count = wide // K
    for start in range(0, col_count, P_BLOCK):
        window = jnp.concatenate([ref[0, start : start + Q_BLOCK, :] for ref in window_refs], axis=0)
        summed = jnp.dot(band_ref[...], window, preferred_element_type=jnp.float32)
        for k in range(K):
            taps_ref[start : start + P_BLOCK, k * chan_count : (k + 1) * chan_count] = summed[
                k * P_BLOCK : (k + 1) * P_BLOCK
            ].astype(jnp.bfloat16)


def pack_row(row, place, place_ref, store):
    count, half, wide = place_ref.shape
    share = wide // 2
    for d in range(count):
        place_ref[d] = jnp.concatenate(
            [row[:half, d * share : (d + 1) * share], row[half:, d * share : (d + 1) * share]], axis=1
        )
    for s in range(count):
        store(s, place_ref[lax.rem(place + s, count)].astype(jnp.bfloat16))


def unpack_row(pieces, place, place_ref):
    count, half, wide = place_ref.shape
    share = wide // 2
    for s in range(count):
        place_ref[lax.rem(place + s, count)] = pieces[s].astype(jnp.float32)
    parts = []
    for d in range(count):
        piece = place_ref[d]
        parts.append(jnp.concatenate([piece[:, :share], piece[:, share:]], axis=0))
    return jnp.concatenate(parts, axis=1)


def pack_kernel(place_ref, row_ref, *refs):
    outs, scratch = refs[:-1], refs[-1]

    def store(s, piece):
        outs[s][0] = piece

    pack_row(row_ref[0].astype(jnp.float32), place_ref[0], scratch, store)


SMEM_SPEC = pl.BlockSpec(memory_space=pltpu.SMEM)


def pack_call(place, field, lon_count, first, count):
    cols, chans = field.shape[1:]
    half, wide = cols // 2, 2 * (chans // lon_count)
    return pl.pallas_call(
        pack_kernel,
        grid=(count,),
        in_specs=[SMEM_SPEC, pl.BlockSpec((1, cols, chans), lambda t: (t + first, 0, 0))],
        out_specs=[pl.BlockSpec((1, half, wide), lambda t: (t, 0, 0))] * lon_count,
        out_shape=[jax.ShapeDtypeStruct((count, half, wide), jnp.bfloat16)] * lon_count,
        scratch_shapes=[pltpu.VMEM((lon_count, half, wide), jnp.float32)],
        compiler_params=pltpu.CompilerParams(vmem_limit_bytes=VMEM_LIMIT),
        cost_estimate=cost(0.6 * count),
    )(place, field)


def conv_kernel(lon_count, place_ref, coef_ref, w0, w1, w2, w3, w4, weight_ref, *refs):
    conv_ref, outs = refs[-4 - lon_count], refs[-3 - lon_count : -3]
    scratch, band_ref, taps_ref = refs[-3:]
    fill_taps(coef_ref, (w0, w1, w2, w3, w4), band_ref, taps_ref)
    conv = jnp.dot(taps_ref[...], weight_ref[...], preferred_element_type=jnp.float32).astype(jnp.bfloat16)
    conv_ref[0] = conv
    hidden = gelu_value(conv.astype(jnp.float32))

    def store(s, piece):
        outs[s][0] = piece

    pack_row(hidden, place_ref[0], scratch, store)


def back_kernel(added, coef_ref, w0, w1, w2, w3, w4, weight_ref, source_ref, *refs):
    input_ref, weight_grad_ref, band_ref, taps_ref = refs[-4:]
    fill_taps(coef_ref, (w0, w1, w2, w3, w4), band_ref, taps_ref)
    input_ref[0] = jnp.dot(
        taps_ref[...], weight_ref[...], preferred_element_type=jnp.float32
    ).astype(jnp.bfloat16)

    @pl.when(pl.program_id(0) == 0)
    def _():
        if added:
            weight_grad_ref[...] = refs[1][...]
        else:
            weight_grad_ref[...] = jnp.zeros_like(weight_grad_ref)

    weight_grad_ref[...] += lax.dot_general(
        source_ref[0], taps_ref[...], (((0,), (0,)), ((), ())), preferred_element_type=jnp.float32
    )


def tap_specs(padded, coefs, flat_weight, first):
    wide_count, chan_count = padded.shape[1:]

    def window_spec(place):
        return pl.BlockSpec((1, wide_count, chan_count), lambda t: (t + first + place, 0, 0))

    in_specs = [pl.BlockSpec((1,) + coefs.shape[1:], lambda t: (t + first, 0, 0))]
    in_specs += [window_spec(place) for place in range(N_LAT_TAPS)]
    in_specs += [pl.BlockSpec(flat_weight.shape, lambda t: (0, 0))]
    return in_specs, [coefs] + [padded] * N_LAT_TAPS + [flat_weight]


def tap_scratch(col_count, chan_count):
    return [
        pltpu.VMEM((K * P_BLOCK, N_LAT_TAPS * Q_BLOCK), jnp.bfloat16),
        pltpu.VMEM((col_count, K * chan_count), jnp.bfloat16),
    ]


def conv_call(place, padded, coefs, flat_weight, col_count, lon_count, first, row_count, held):
    chan_count = padded.shape[2]
    half, wide = col_count // 2, 2 * (chan_count // lon_count)
    in_specs, operands = tap_specs(padded, coefs, flat_weight, first)
    out_specs = [pl.BlockSpec((1, col_count, chan_count), lambda t: (t + first, 0, 0))]
    out_specs += [pl.BlockSpec((1, half, wide), lambda t: (t, 0, 0))] * lon_count
    out_shape = [jax.ShapeDtypeStruct((coefs.shape[0], col_count, chan_count), jnp.bfloat16)]
    aliases = {}
    if held is not None:
        aliases = {len(operands) + 1: 0}
        in_specs.append(pl.BlockSpec(memory_space=pl.ANY))
        operands.append(held)
    out_shape += [jax.ShapeDtypeStruct((row_count, half, wide), jnp.bfloat16)] * lon_count
    outs = pl.pallas_call(
        functools.partial(conv_kernel, lon_count),
        grid=(row_count,),
        in_specs=[SMEM_SPEC] + in_specs,
        out_specs=out_specs,
        out_shape=out_shape,
        scratch_shapes=[pltpu.VMEM((lon_count, half, wide), jnp.float32)]
        + tap_scratch(col_count, chan_count),
        compiler_params=pltpu.CompilerParams(vmem_limit_bytes=VMEM_LIMIT),
        input_output_aliases=aliases,
        cost_estimate=cost(2.0 * row_count),
    )(place, *operands)
    return outs[0], outs[1:]


def back_call(padded, coefs, flat_weight, source, first, row_count, held):
    total_rows, col_count, chan_count = source.shape
    in_specs, operands = tap_specs(padded, coefs, flat_weight, first)
    row_spec = pl.BlockSpec((1, col_count, chan_count), lambda t: (t + first, 0, 0))
    row_shape = jax.ShapeDtypeStruct((total_rows, col_count, chan_count), jnp.bfloat16)
    grad_shape = (chan_count, K * chan_count)
    grad_spec = pl.BlockSpec(grad_shape, lambda t: (0, 0))
    in_specs.append(row_spec)
    operands.append(source)
    aliases = {}
    if held is not None:
        aliases = {len(operands): 0}
        in_specs += [pl.BlockSpec(memory_space=pl.ANY), grad_spec]
        operands += list(held)
    return pl.pallas_call(
        functools.partial(back_kernel, held is not None),
        grid=(row_count,),
        in_specs=in_specs,
        out_specs=(row_spec, grad_spec),
        out_shape=(row_shape, jax.ShapeDtypeStruct(grad_shape, jnp.float32)),
        scratch_shapes=tap_scratch(col_count, chan_count),
        input_output_aliases=aliases,
        compiler_params=pltpu.CompilerParams(vmem_limit_bytes=VMEM_LIMIT),
        cost_estimate=cost(2.4 * row_count),
    )(*operands)


def dft_kernel(scaled, lon_count, starts, table_ref, quad_ref, *refs):
    pieces, out_ref, wide_ref = refs[:-2], refs[-2], refs[-1]
    share = pieces[0].shape[2] // 2
    group, t = pl.program_id(0), pl.program_id(1)
    rows = []
    for s in range(lon_count):
        piece = pieces[s][0]
        for index, start in enumerate(starts):
            piece = jnp.where(group < start, piece, pieces[(index + 1) * lon_count + s][0])
        rows += [piece[:, :share], piece[:, share:]]
    spectrum = jnp.dot(table_ref[...], jnp.concatenate(rows, axis=0), preferred_element_type=jnp.float32)
    orders = spectrum.shape[0] // 2
    lines = jnp.concatenate([spectrum[:orders], spectrum[orders:]], axis=1)
    if scaled:
        lines = lines * quad_ref[0]
    for start, size in lane_tiles(2 * share):
        tile = lines[:, start : start + size]
        if size < LANES:
            tile = jnp.pad(tile, ((0, 0), (0, LANES - size)))
        wide_ref[start // LANES, pl.ds(t, orders, stride=GROUP), :] = tile

    @pl.when(t == GROUP - 1)
    def _():
        blocks, held = out_ref.shape[:2]
        step = held * GROUP
        for b in range(blocks):
            for start, size in lane_tiles(2 * share):
                block = wide_ref[start // LANES, b * step : (b + 1) * step, :size]
                out_ref[b, :, :, start : start + size] = block.reshape(held, GROUP, size).astype(
                    jnp.bfloat16
                )


def dft_call(table, quad_rows, chunks, first, lat_count, scaled):
    lon_count = len(chunks[0])
    half, wide = chunks[0][0].shape[1:]
    held = table.shape[0] // (2 * lat_count)

    def piece_spec(start, count):
        return pl.BlockSpec(
            (1, half, wide), lambda g, t: (jnp.clip(g * GROUP + t - start, 0, count - 1), 0, 0)
        )

    piece_specs, starts, rows = [], [], 0
    for pieces in chunks:
        if rows:
            starts.append(rows // GROUP)
        piece_specs += [piece_spec(rows, pieces[0].shape[0])] * lon_count
        rows += pieces[0].shape[0]
    return pl.pallas_call(
        functools.partial(dft_kernel, scaled, lon_count, starts),
        grid=(rows // GROUP, GROUP),
        in_specs=[
            pl.BlockSpec(table.shape, lambda g, t: (0, 0)),
            pl.BlockSpec((1, 1, wide), lambda g, t: (first + g * GROUP + t, 0, 0)),
        ]
        + piece_specs,
        out_specs=pl.BlockSpec((lat_count, held, GROUP, wide), lambda g, t: (0, 0, g, 0)),
        out_shape=jax.ShapeDtypeStruct((lat_count, held, rows, wide), jnp.bfloat16),
        scratch_shapes=[wide_scratch(lat_count * held * GROUP, wide)],
        compiler_params=pltpu.CompilerParams(vmem_limit_bytes=VMEM_LIMIT),
        cost_estimate=cost(0.9 * rows),
    )(table, quad_rows, *[piece for pieces in chunks for piece in pieces])


def idft_kernel(lon_count, table_ref, wide_in_ref, *refs):
    outs, wide_ref = refs[:lon_count], refs[lon_count]
    wide = wide_in_ref.shape[3]
    t = pl.program_id(1)

    @pl.when(t == 0)
    def _():
        blocks, held = wide_in_ref.shape[:2]
        step = held * GROUP
        for b in range(blocks):
            for start, size in lane_tiles(wide):
                block = wide_in_ref[b, :, :, start : start + size]
                wide_ref[start // LANES, b * step : (b + 1) * step, :size] = block.astype(
                    jnp.float32
                ).reshape(step, size)

    orders = wide_ref.shape[1] // GROUP
    tiles = []
    for start, size in lane_tiles(wide):
        tiles.append(wide_ref[start // LANES, pl.ds(t, orders, stride=GROUP), :][:, :size])
    lines = jnp.concatenate(tiles, axis=1).astype(jnp.bfloat16)
    share = wide // 2
    stacked = jnp.concatenate([lines[:, :share], lines[:, share:]], axis=0)
    grid_rows = jnp.dot(table_ref[...], stacked, preferred_element_type=jnp.float32)
    half = grid_rows.shape[0] // (2 * lon_count)
    for s in range(lon_count):
        start = 2 * s * half
        outs[s][0] = jnp.concatenate(
            [grid_rows[start : start + half], grid_rows[start + half : start + 2 * half]], axis=1
        ).astype(jnp.bfloat16)


def idft_call(table, received, lon_count, first, count):
    lat_count, held, _, wide = received.shape
    start = first // GROUP
    half = table.shape[0] // (2 * lon_count)
    return pl.pallas_call(
        functools.partial(idft_kernel, lon_count),
        grid=(count // GROUP, GROUP),
        in_specs=[
            pl.BlockSpec(table.shape, lambda g, t: (0, 0)),
            pl.BlockSpec((lat_count, held, GROUP, wide), lambda g, t: (0, 0, g + start, 0)),
        ],
        out_specs=[pl.BlockSpec((1, half, wide), lambda g, t: (g * GROUP + t, 0, 0))] * lon_count,
        out_shape=[jax.ShapeDtypeStruct((count, half, wide), jnp.bfloat16)] * lon_count,
        scratch_shapes=[wide_scratch(lat_count * held * GROUP, wide)],
        compiler_params=pltpu.CompilerParams(vmem_limit_bytes=VMEM_LIMIT),
        cost_estimate=cost(0.8 * count),
    )(table, received)


def legendre_kernel(spectral_count, forward, table_ref, gain_ref, quad_ref, *refs):
    ins = refs[:spectral_count]
    refs = refs[spectral_count:]
    table = table_ref[0]
    rows = jnp.concatenate([ref[:, 0].astype(jnp.float32) for ref in ins], axis=1)
    lat_total, wide = rows.shape[0] * rows.shape[1], rows.shape[2]
    spectral = rows.reshape(lat_total, wide).astype(jnp.bfloat16)
    coefs = jnp.dot(table, spectral, preferred_element_type=jnp.float32)
    if forward:
        cot_ref, outs, sum_ref = refs[0], refs[1:-1], refs[-1]

        @pl.when(pl.program_id(0) == 0)
        def _():
            sum_ref[...] = jnp.zeros_like(sum_ref)

        sum_ref[...] += coefs * cot_ref[0]
    else:
        outs = refs[:-1]
        refs[-1][0] = coefs
    filtered = (gain_ref[...] * coefs).astype(jnp.bfloat16)
    synth = lax.dot_general(
        table, filtered, (((0,), (0,)), ((), ())), preferred_element_type=jnp.float32
    )
    if not forward:
        synth = synth * quad_ref[...]
    synth = synth.reshape(rows.shape)
    start = 0
    for ref in outs:
        count = ref.shape[2]
        ref[:, 0] = synth[:, start : start + count].astype(jnp.bfloat16)
        start += count


def legendre_call(table, gain, quad_all, received, spans, cot_coefs):
    lat_count, held, _, wide = received[0].shape
    degrees, lat_total = table.shape[1:]
    forward = cot_coefs is not None

    def chunk_spec(count):
        return pl.BlockSpec((lat_count, 1, count, wide), lambda i: (0, i, 0, 0))

    coef_spec = pl.BlockSpec((1, degrees, wide), lambda i: (i, 0, 0))
    in_specs = [
        pl.BlockSpec((1, degrees, lat_total), lambda i: (i, 0, 0)),
        pl.BlockSpec(gain.shape, lambda i: (0, 0)),
        pl.BlockSpec(quad_all.shape, lambda i: (0, 0)),
    ] + [chunk_spec(chunk.shape[2]) for chunk in received]
    operands = [table, gain, quad_all] + list(received)
    out_specs = [chunk_spec(count) for _, count in spans]
    out_shape = [
        jax.ShapeDtypeStruct((lat_count, held, count, wide), jnp.bfloat16) for _, count in spans
    ]
    if forward:
        in_specs.append(coef_spec)
        operands.append(cot_coefs)
        out_specs.append(pl.BlockSpec((degrees, wide), lambda i: (0, 0)))
        out_shape.append(jax.ShapeDtypeStruct((degrees, wide), jnp.float32))
    else:
        out_specs.append(coef_spec)
        out_shape.append(jax.ShapeDtypeStruct((held, degrees, wide), jnp.float32))
    outs = pl.pallas_call(
        functools.partial(legendre_kernel, len(received), forward),
        grid=(held,),
        in_specs=in_specs,
        out_specs=out_specs,
        out_shape=out_shape,
        compiler_params=pltpu.CompilerParams(vmem_limit_bytes=VMEM_LIMIT),
        cost_estimate=cost(1.1 * held),
    )(*operands)
    return outs[:-1], outs[-1]


def cot_conv_kernel(lon_count, place_ref, conv_ref, cot_ref, *refs):
    pieces, out_ref, scratch = refs[:lon_count], refs[-2], refs[-1]
    cot_hidden = unpack_row([ref[0] for ref in pieces], place_ref[0], scratch)
    slope = gelu_slope(conv_ref[0].astype(jnp.float32))
    out_ref[0] = (cot_ref[0].astype(jnp.float32) + cot_hidden * slope).astype(jnp.bfloat16)


def result_kernel(lon_count, place_ref, conv_ref, *refs):
    pieces, out_ref, scratch = refs[:lon_count], refs[-2], refs[-1]
    branch = unpack_row([ref[0] for ref in pieces], place_ref[0], scratch)
    out_ref[0] = (conv_ref[0].astype(jnp.float32) + branch).astype(jnp.bfloat16)


def grid_call(kernel, place, conv_out, beside, pieces, first, count, held):
    lon_count = len(pieces)
    cols, chans = conv_out.shape[1:]
    half, wide = pieces[0].shape[1:]
    row_spec = pl.BlockSpec((1, cols, chans), lambda t: (t + first, 0, 0))
    piece_spec = pl.BlockSpec((1, half, wide), lambda t: (t, 0, 0))
    in_specs = [SMEM_SPEC, row_spec] + [row_spec] * len(beside) + [piece_spec] * lon_count
    operands = [place, conv_out] + beside + list(pieces)
    aliases = {}
    if held is not None:
        aliases = {len(operands): 0}
        in_specs.append(pl.BlockSpec(memory_space=pl.ANY))
        operands.append(held)
    return pl.pallas_call(
        functools.partial(kernel, lon_count),
        grid=(count,),
        in_specs=in_specs,
        out_specs=row_spec,
        out_shape=jax.ShapeDtypeStruct(conv_out.shape, jnp.bfloat16),
        scratch_shapes=[pltpu.VMEM((lon_count, half, wide), jnp.float32)],
        input_output_aliases=aliases,
        compiler_params=pltpu.CompilerParams(vmem_limit_bytes=VMEM_LIMIT),
        cost_estimate=cost(0.9 * count),
    )(*operands)


def edges(block, axis, dim, width, periodic):
    count = lax.axis_size(axis)
    forward = [(i, i + 1) for i in range(count - 1)]
    if periodic:
        forward.append((count - 1, 0))
    backward = [(target, source) for source, target in forward]
    size = block.shape[dim]
    low = lax.ppermute(lax.slice_in_dim(block, size - width, size, axis=dim), axis, forward)
    high = lax.ppermute(lax.slice_in_dim(block, 0, width, axis=dim), axis, backward)
    return low, high


def padded_field(field, lat_edges, *gates):
    low, high = lat_edges
    cols = field.shape[1]
    ends = jnp.concatenate(
        [jnp.concatenate([part[:, :DW], part[:, cols - DW :]], axis=1) for part in (low, field, high)],
        axis=0,
    )
    west, east = edges(ends, "lon", 1, DW, True)
    tall = jnp.concatenate([low, after(field, *gates), high], axis=0)
    margin = jnp.zeros((tall.shape[0], Q_BLOCK - P_BLOCK - 2 * DW, tall.shape[2]), field.dtype)
    return jnp.concatenate([west, tall, east, margin], axis=1)


def after(value, *earlier):
    return lax.optimization_barrier((value,) + earlier)[0]


def swap(pieces, direction, earlier=None):
    count = lax.axis_size("lon")
    moved = [pieces[0]]
    for s in range(1, count):
        perm = [(i, (i + direction * s) % count) for i in range(count)]
        sent = pieces[s] if earlier is None else after(pieces[s], earlier)
        moved.append(lax.ppermute(sent, "lon", perm))
    return moved


def over_lat(blocks):
    return lax.all_to_all(blocks, "lat", split_axis=0, concat_axis=0, tiled=True)


def summed_everywhere(terms, gain_terms, gates, later_gate):
    lat_count, lon_count = lax.axis_size("lat"), lax.axis_size("lon")
    wide = terms.shape[1]
    parts = jnp.concatenate([terms, gain_terms], axis=1).astype(jnp.bfloat16)
    parts = parts.reshape(lat_count, -1, parts.shape[1])
    own = jnp.sum(over_lat(after(parts, *gates)).astype(jnp.float32), axis=0)
    pieces = jnp.stack(swap([own] * lon_count, 1))
    places = (lax.axis_index("lon") - jnp.arange(lon_count, dtype=jnp.int32)) % lon_count
    pieces = pieces[places]
    gains = [pieces[d, :, wide:] for d in range(lon_count)]
    total = jnp.concatenate([jnp.sum(pieces[:, :, :wide], axis=0)] + gains, axis=1).astype(jnp.bfloat16)
    shares = over_lat(after(jnp.broadcast_to(total[None], (lat_count,) + total.shape), later_gate))
    shares = shares.reshape(terms.shape[0], -1).astype(jnp.float32)
    return shares[:, :wide], shares[:, wide:]


def spans_of(*counts):
    spans, first = [], 0
    for count in counts:
        spans.append((first, count))
        first += count
    return spans


def body(
    source_field,
    cotangent,
    weight,
    spectral_gain,
    legendre,
    support_lat,
    support_lon,
    support_val,
    order_map,
):
    row_count, col_count, chan_count = source_field.shape
    lon_count, lat_count = lax.axis_size("lon"), lax.axis_size("lat")
    lat_total = row_count * lat_count
    band_index = lax.axis_index("lat")
    block_index = lax.axis_index("lon")
    share = chan_count // lon_count
    place = block_index.astype(jnp.int32).reshape(1)
    third = row_count // 3
    thirds = spans_of(third, third, row_count - 2 * third)
    spans = spans_of(row_count - third, third)

    back_places = (block_index - jnp.arange(lon_count, dtype=jnp.int32)) % lon_count
    longitude = (back_places[:, None] * col_count + jnp.arange(col_count, dtype=jnp.int32)).reshape(-1)
    orders = jnp.take(order_map.reshape(lat_count, lon_count, -1), back_places, axis=1).reshape(-1)
    inverse_table = dft_table(longitude, orders)
    forward_table = inverse_table.T
    all_rows = jnp.arange(lat_total, dtype=jnp.int32).astype(jnp.float32)
    quad_all = jnp.sin(math.pi * (all_rows + 0.5) / lat_total)
    quad_band = lax.dynamic_slice_in_dim(quad_all, band_index * row_count, row_count, 0)
    quad_rows = jnp.broadcast_to(quad_band[:, None, None], (row_count, 1, 2 * share))
    gain = lax.dynamic_slice_in_dim(spectral_gain, block_index * share, share, 1)
    gain = jnp.concatenate([gain, gain], axis=1)
    tap_weights = tap_table(support_lat, support_lon, support_val)
    tap_pad = jnp.pad(tap_weights, ((H, H), (0, 0), (0, 0), (0, 0)))
    tap_rows = lax.dynamic_slice_in_dim(tap_pad, band_index * row_count, row_count + 2 * H, 0)
    flat_weight = weight.reshape(K * chan_count, chan_count)
    flat_weight_back = weight.transpose(0, 2, 1).reshape(K * chan_count, chan_count)

    coefs = tap_coefficients(tap_rows, row_count, False)

    source_edges = edges(source_field, "lat", 0, H, False)
    packed = [pack_call(place, cotangent, lon_count, first, count) for first, count in thirds]
    padded_source, conv_out, hidden_pieces, last = None, None, [], None
    gates, cot_received, sent_gates = [pieces[0] for pieces in packed], [], source_edges
    for (first, count), pieces in zip(thirds, packed):
        lines = swap(pieces, 1, last)
        last = lines[-1]
        blocks = dft_call(
            forward_table, quad_rows, [[after(lines[0], *gates)] + lines[1:]], first, lat_count, False
        )
        cot_received.append(over_lat(after(blocks, *sent_gates)))
        sent_gates = [cot_received[-1]]
        if padded_source is None:
            padded_source = padded_field(source_field, source_edges, blocks)
        conv_out, pieces = conv_call(
            place, after(padded_source, blocks), coefs, flat_weight, col_count, lon_count, first, count, conv_out
        )
        gates = [conv_out]
        hidden_pieces.append(pieces)
    hidden_lines = []
    for pieces in hidden_pieces:
        hidden_lines.append(swap(pieces, 1, last))
        last = hidden_lines[-1][-1]
    table = jnp.concatenate(swap([legendre] * lon_count, 1, last), axis=0)
    hidden_blocks = dft_call(forward_table, quad_rows, hidden_lines, 0, lat_count, True)
    hidden_received = over_lat(after(hidden_blocks, cot_received[-1]))

    quad_column = quad_all[:, None]
    cot_synth, cot_coefs = legendre_call(
        after(table, hidden_blocks), gain, quad_column, cot_received, spans, None
    )
    synth, gain_terms = legendre_call(table, gain, quad_column, [hidden_received], spans, cot_coefs)
    first_back = over_lat(after(cot_synth[0], hidden_received))
    second_back = over_lat(after(cot_synth[1], first_back, synth[0]))
    cot_pieces = [swap(idft_call(inverse_table, after(first_back, synth[0]), lon_count, 0, third), -1)]
    last = cot_pieces[0][-1]
    first_branch = over_lat(after(synth[0], second_back, last))
    rest = row_count - 2 * third
    cot_pieces.append(
        swap(idft_call(inverse_table, after(first_back, last), lon_count, third, rest), -1, last)
    )
    last = cot_pieces[1][-1]
    cot_pieces.append(swap(idft_call(inverse_table, second_back, lon_count, 0, third), -1, last))
    cot_conv = None
    for (first, count), pieces in zip(spans_of(third, rest, third), cot_pieces):
        cot_conv = grid_call(
            cot_conv_kernel, place, conv_out, [cotangent], pieces, first, count, cot_conv
        )
    cot_edges = edges(cot_conv, "lat", 0, H, False)
    second_branch = over_lat(after(synth[1], first_branch, *cot_edges))
    padded_cot = padded_field(cot_conv, cot_edges)
    coefs_back = tap_coefficients(tap_rows, row_count, True)
    lines = idft_call(inverse_table, after(first_branch, padded_cot), lon_count, 0, row_count - third)
    first_lines = swap(lines, -1)
    padded_cot = after(padded_cot, lines[0])
    back = None
    for first, count in spans:
        back = back_call(padded_cot, coefs_back, flat_weight_back, source_field, first, count, back)
    grad_input, weight_part = back

    second_lines = idft_call(inverse_table, after(second_branch, grad_input), lon_count, 0, third)
    gates = [second_branch, first_lines[-1], second_lines[0]]
    second_lines = swap(second_lines, -1, first_lines[-1])
    result = None
    for (first, count), pieces in zip(spans, [first_lines, second_lines]):
        result = grid_call(result_kernel, place, conv_out, [], pieces, first, count, result)

    gain_part = gain_terms[:, :share] + gain_terms[:, share:]
    weight_total, gain_total = summed_everywhere(weight_part, gain_part, gates, second_lines[-1])
    weight_total = weight_total.reshape(chan_count, K, chan_count)
    grad_weight = weight_total.transpose(1, 0, 2) / math.sqrt(1.0 * lat_total * NLON)
    grad_gain = gain_total / math.sqrt(2.0 * M)
    return (result, grad_input, grad_weight, grad_gain)


def solution(mesh):
    return jax.shard_map(
        body,
        mesh=mesh,
        in_specs=(
            P("lat", "lon", None),
            P("lat", "lon", None),
            P(),
            P(),
            P(("lat", "lon"), None, None),
            P(),
            P(),
            P(),
            P(),
        ),
        out_specs=(P("lat", "lon", None), P("lat", "lon", None), P(), P()),
        check_vma=False,
    )
```

```python
import functools
import math

import jax
import jax.numpy as jnp
from jax import lax
from jax.experimental import pallas as pl
from jax.experimental.pallas import tpu as pltpu
from jax.sharding import PartitionSpec as P

NLON = 768
M = 384
K = 3
H = 2
DW = 4


SQRT_HALF = 0.7071067811865476
INV_SQRT_TAU = 0.3989422804014327


def gelu_value(values):
    return 0.5 * values * (1.0 + lax.erf(values * SQRT_HALF))


def gelu_slope(values):
    return 0.5 * (1.0 + lax.erf(values * SQRT_HALF)) + values * INV_SQRT_TAU * jnp.exp(
        -0.5 * values * values
    )


def tap_table(support_lat, support_lon, support_val):
    lat_steps = jnp.arange(2 * H + 1, dtype=jnp.int32) - H
    lon_steps = jnp.arange(2 * DW + 1, dtype=jnp.int32) - DW
    lat_onehot = (support_lat[:, :, None] == lat_steps[None, None, :]).astype(jnp.float32)
    lon_onehot = (support_lon[:, :, None] == lon_steps[None, None, :]).astype(jnp.float32)
    return jnp.einsum(
        "tsk,tsa,tsd->tkad", support_val, lat_onehot, lon_onehot, precision=lax.Precision.HIGHEST
    )


def dft_table(longitude, frequency):
    cycles = longitude[:, None] * frequency[None, :] % NLON
    angles = cycles.astype(jnp.float32) * (2.0 * math.pi / NLON)
    matrix = jnp.concatenate([jnp.cos(angles), -jnp.sin(angles)], axis=1) * math.sqrt(2.0 / NLON)
    return matrix.astype(jnp.bfloat16)


P_BLOCK = 96
Q_BLOCK = 128
N_LAT_TAPS = 2 * H + 1
VMEM_LIMIT = 48 * 1024 * 1024
GROUP = 8
LANES = 128
WEST = 8


def lane_tiles(wide):
    return [(start, min(LANES, wide - start)) for start in range(0, wide, LANES)]


def wide_scratch(rows, wide):
    return pltpu.VMEM((len(lane_tiles(wide)), rows, LANES), jnp.float32)


def cost(micros):
    return pl.CostEstimate(
        flops=int(micros * 6e8), bytes_accessed=int(micros * 2e6), transcendentals=0
    )


def tap_coefficients(tap_rows, row_count, mirror):
    coef_list = []
    for place in range(N_LAT_TAPS):
        if mirror:
            taken = tap_rows[place : place + row_count, :, N_LAT_TAPS - 1 - place, ::-1]
        else:
            taken = tap_rows[H : H + row_count, :, place, :]
        coef_list.append(taken)
    coefs = jnp.stack(coef_list, axis=2).reshape(row_count, K * N_LAT_TAPS, 2 * DW + 1)
    return jnp.pad(coefs, ((0, 0), (0, 1), (WEST - DW, Q_BLOCK - WEST - DW - 1)))


def fill_taps(coef_ref, window_refs, band_ref, taps_ref):
    for k in range(K):
        for place in range(N_LAT_TAPS):
            index = k * N_LAT_TAPS + place
            row = jnp.broadcast_to(coef_ref[0, index : index + 1, :], (P_BLOCK, Q_BLOCK))
            band = pltpu.roll(row, 0, 1, stride=1, stride_axis=0)
            band_ref[
                k * P_BLOCK : (k + 1) * P_BLOCK, place * Q_BLOCK : (place + 1) * Q_BLOCK
            ] = band.astype(jnp.bfloat16)
    col_count, wide = taps_ref.shape
    chan_count = wide // K
    for start in range(0, col_count, P_BLOCK):
        window = jnp.concatenate([ref[0, start : start + Q_BLOCK, :] for ref in window_refs], axis=0)
        summed = jnp.dot(band_ref[...], window, preferred_element_type=jnp.float32)
        for k in range(K):
            taps_ref[start : start + P_BLOCK, k * chan_count : (k + 1) * chan_count] = summed[
                k * P_BLOCK : (k + 1) * P_BLOCK
            ].astype(jnp.bfloat16)


def pack_row(row, place, place_ref, store):
    count, half, wide = place_ref.shape
    share = wide // 2
    for d in range(count):
        place_ref[d] = jnp.concatenate(
            [row[:half, d * share : (d + 1) * share], row[half:, d * share : (d + 1) * share]], axis=1
        )
    for s in range(count):
        store(s, place_ref[lax.rem(place + s, count)].astype(jnp.bfloat16))


def unpack_row(pieces, place, place_ref):
    count, half, wide = place_ref.shape
    share = wide // 2
    for s in range(count):
        place_ref[lax.rem(place + s, count)] = pieces[s].astype(jnp.float32)
    parts = []
    for d in range(count):
        piece = place_ref[d]
        parts.append(jnp.concatenate([piece[:, :share], piece[:, share:]], axis=0))
    return jnp.concatenate(parts, axis=1)


def pack_kernel(place_ref, row_ref, *refs):
    outs, scratch = refs[:-1], refs[-1]

    def store(s, piece):
        outs[s][0] = piece

    pack_row(row_ref[0].astype(jnp.float32), place_ref[0], scratch, store)


SMEM_SPEC = pl.BlockSpec(memory_space=pltpu.SMEM)


def pack_call(place, field, lon_count, first, count):
    cols, chans = field.shape[1:]
    half, wide = cols // 2, 2 * (chans // lon_count)
    return pl.pallas_call(
        pack_kernel,
        grid=(count,),
        in_specs=[SMEM_SPEC, pl.BlockSpec((1, cols, chans), lambda t: (t + first, 0, 0))],
        out_specs=[pl.BlockSpec((1, half, wide), lambda t: (t, 0, 0))] * lon_count,
        out_shape=[jax.ShapeDtypeStruct((count, half, wide), jnp.bfloat16)] * lon_count,
        scratch_shapes=[pltpu.VMEM((lon_count, half, wide), jnp.float32)],
        compiler_params=pltpu.CompilerParams(vmem_limit_bytes=VMEM_LIMIT),
        cost_estimate=cost(0.6 * count),
    )(place, field)


def conv_kernel(lon_count, place_ref, coef_ref, w0, w1, w2, w3, w4, weight_ref, *refs):
    conv_ref, outs = refs[-4 - lon_count], refs[-3 - lon_count : -3]
    scratch, band_ref, taps_ref = refs[-3:]
    fill_taps(coef_ref, (w0, w1, w2, w3, w4), band_ref, taps_ref)
    conv = jnp.dot(taps_ref[...], weight_ref[...], preferred_element_type=jnp.float32).astype(jnp.bfloat16)
    conv_ref[0] = conv
    hidden = gelu_value(conv.astype(jnp.float32))

    def store(s, piece):
        outs[s][0] = piece

    pack_row(hidden, place_ref[0], scratch, store)


def back_kernel(added, coef_ref, w0, w1, w2, w3, w4, weight_ref, source_ref, *refs):
    input_ref, weight_grad_ref, band_ref, taps_ref = refs[-4:]
    fill_taps(coef_ref, (w0, w1, w2, w3, w4), band_ref, taps_ref)
    input_ref[0] = jnp.dot(
        taps_ref[...], weight_ref[...], preferred_element_type=jnp.float32
    ).astype(jnp.bfloat16)

    @pl.when(pl.program_id(0) == 0)
    def _():
        if added:
            weight_grad_ref[...] = refs[1][...]
        else:
            weight_grad_ref[...] = jnp.zeros_like(weight_grad_ref)

    weight_grad_ref[...] += lax.dot_general(
        source_ref[0], taps_ref[...], (((0,), (0,)), ((), ())), preferred_element_type=jnp.float32
    )


def tap_specs(padded, coefs, flat_weight, first):
    wide_count, chan_count = padded.shape[1:]

    def window_spec(place):
        return pl.BlockSpec((1, wide_count, chan_count), lambda t: (t + first + place, 0, 0))

    in_specs = [pl.BlockSpec((1,) + coefs.shape[1:], lambda t: (t + first, 0, 0))]
    in_specs += [window_spec(place) for place in range(N_LAT_TAPS)]
    in_specs += [pl.BlockSpec(flat_weight.shape, lambda t: (0, 0))]
    return in_specs, [coefs] + [padded] * N_LAT_TAPS + [flat_weight]


def tap_scratch(col_count, chan_count):
    return [
        pltpu.VMEM((K * P_BLOCK, N_LAT_TAPS * Q_BLOCK), jnp.bfloat16),
        pltpu.VMEM((col_count, K * chan_count), jnp.bfloat16),
    ]


def conv_call(place, padded, coefs, flat_weight, col_count, lon_count, first, row_count, held):
    chan_count = padded.shape[2]
    half, wide = col_count // 2, 2 * (chan_count // lon_count)
    in_specs, operands = tap_specs(padded, coefs, flat_weight, first)
    out_specs = [pl.BlockSpec((1, col_count, chan_count), lambda t: (t + first, 0, 0))]
    out_specs += [pl.BlockSpec((1, half, wide), lambda t: (t, 0, 0))] * lon_count
    out_shape = [jax.ShapeDtypeStruct((coefs.shape[0], col_count, chan_count), jnp.bfloat16)]
    aliases = {}
    if held is not None:
        aliases = {len(operands) + 1: 0}
        in_specs.append(pl.BlockSpec(memory_space=pl.ANY))
        operands.append(held)
    out_shape += [jax.ShapeDtypeStruct((row_count, half, wide), jnp.bfloat16)] * lon_count
    outs = pl.pallas_call(
        functools.partial(conv_kernel, lon_count),
        grid=(row_count,),
        in_specs=[SMEM_SPEC] + in_specs,
        out_specs=out_specs,
        out_shape=out_shape,
        scratch_shapes=[pltpu.VMEM((lon_count, half, wide), jnp.float32)]
        + tap_scratch(col_count, chan_count),
        compiler_params=pltpu.CompilerParams(vmem_limit_bytes=VMEM_LIMIT),
        input_output_aliases=aliases,
        cost_estimate=cost(2.0 * row_count),
    )(place, *operands)
    return outs[0], outs[1:]


def back_call(padded, coefs, flat_weight, source, first, row_count, held):
    total_rows, col_count, chan_count = source.shape
    in_specs, operands = tap_specs(padded, coefs, flat_weight, first)
    row_spec = pl.BlockSpec((1, col_count, chan_count), lambda t: (t + first, 0, 0))
    row_shape = jax.ShapeDtypeStruct((total_rows, col_count, chan_count), jnp.bfloat16)
    grad_shape = (chan_count, K * chan_count)
    grad_spec = pl.BlockSpec(grad_shape, lambda t: (0, 0))
    in_specs.append(row_spec)
    operands.append(source)
    aliases = {}
    if held is not None:
        aliases = {len(operands): 0}
        in_specs += [pl.BlockSpec(memory_space=pl.ANY), grad_spec]
        operands += list(held)
    return pl.pallas_call(
        functools.partial(back_kernel, held is not None),
        grid=(row_count,),
        in_specs=in_specs,
        out_specs=(row_spec, grad_spec),
        out_shape=(row_shape, jax.ShapeDtypeStruct(grad_shape, jnp.float32)),
        scratch_shapes=tap_scratch(col_count, chan_count),
        input_output_aliases=aliases,
        compiler_params=pltpu.CompilerParams(vmem_limit_bytes=VMEM_LIMIT),
        cost_estimate=cost(2.4 * row_count),
    )(*operands)


def dft_kernel(scaled, lon_count, starts, table_ref, quad_ref, *refs):
    pieces, out_ref, wide_ref = refs[:-2], refs[-2], refs[-1]
    share = pieces[0].shape[2] // 2
    group, t = pl.program_id(0), pl.program_id(1)
    rows = []
    for s in range(lon_count):
        piece = pieces[s][0]
        for index, start in enumerate(starts):
            piece = jnp.where(group < start, piece, pieces[(index + 1) * lon_count + s][0])
        rows += [piece[:, :share], piece[:, share:]]
    spectrum = jnp.dot(table_ref[...], jnp.concatenate(rows, axis=0), preferred_element_type=jnp.float32)
    orders = spectrum.shape[0] // 2
    lines = jnp.concatenate([spectrum[:orders], spectrum[orders:]], axis=1)
    if scaled:
        lines = lines * quad_ref[0]
    for start, size in lane_tiles(2 * share):
        tile = lines[:, start : start + size]
        if size < LANES:
            tile = jnp.pad(tile, ((0, 0), (0, LANES - size)))
        wide_ref[start // LANES, pl.ds(t, orders, stride=GROUP), :] = tile

    @pl.when(t == GROUP - 1)
    def _():
        blocks, held = out_ref.shape[:2]
        step = held * GROUP
        for b in range(blocks):
            for start, size in lane_tiles(2 * share):
                block = wide_ref[start // LANES, b * step : (b + 1) * step, :size]
                out_ref[b, :, :, start : start + size] = block.reshape(held, GROUP, size).astype(
                    jnp.bfloat16
                )


def dft_call(table, quad_rows, chunks, first, lat_count, scaled):
    lon_count = len(chunks[0])
    half, wide = chunks[0][0].shape[1:]
    held = table.shape[0] // (2 * lat_count)

    def piece_spec(start, count):
        return pl.BlockSpec(
            (1, half, wide), lambda g, t: (jnp.clip(g * GROUP + t - start, 0, count - 1), 0, 0)
        )

    piece_specs, starts, rows = [], [], 0
    for pieces in chunks:
        if rows:
            starts.append(rows // GROUP)
        piece_specs += [piece_spec(rows, pieces[0].shape[0])] * lon_count
        rows += pieces[0].shape[0]
    return pl.pallas_call(
        functools.partial(dft_kernel, scaled, lon_count, starts),
        grid=(rows // GROUP, GROUP),
        in_specs=[
            pl.BlockSpec(table.shape, lambda g, t: (0, 0)),
            pl.BlockSpec((1, 1, wide), lambda g, t: (first + g * GROUP + t, 0, 0)),
        ]
        + piece_specs,
        out_specs=pl.BlockSpec((lat_count, held, GROUP, wide), lambda g, t: (0, 0, g, 0)),
        out_shape=jax.ShapeDtypeStruct((lat_count, held, rows, wide), jnp.bfloat16),
        scratch_shapes=[wide_scratch(lat_count * held * GROUP, wide)],
        compiler_params=pltpu.CompilerParams(vmem_limit_bytes=VMEM_LIMIT),
        cost_estimate=cost(0.9 * rows),
    )(table, quad_rows, *[piece for pieces in chunks for piece in pieces])


def idft_kernel(lon_count, table_ref, wide_in_ref, *refs):
    outs, wide_ref = refs[:lon_count], refs[lon_count]
    wide = wide_in_ref.shape[3]
    t = pl.program_id(1)

    @pl.when(t == 0)
    def _():
        blocks, held = wide_in_ref.shape[:2]
        step = held * GROUP
        for b in range(blocks):
            for start, size in lane_tiles(wide):
                block = wide_in_ref[b, :, :, start : start + size]
                wide_ref[start // LANES, b * step : (b + 1) * step, :size] = block.astype(
                    jnp.float32
                ).reshape(step, size)

    orders = wide_ref.shape[1] // GROUP
    tiles = []
    for start, size in lane_tiles(wide):
        tiles.append(wide_ref[start // LANES, pl.ds(t, orders, stride=GROUP), :][:, :size])
    lines = jnp.concatenate(tiles, axis=1).astype(jnp.bfloat16)
    share = wide // 2
    stacked = jnp.concatenate([lines[:, :share], lines[:, share:]], axis=0)
    grid_rows = jnp.dot(table_ref[...], stacked, preferred_element_type=jnp.float32)
    half = grid_rows.shape[0] // (2 * lon_count)
    for s in range(lon_count):
        start = 2 * s * half
        outs[s][0] = jnp.concatenate(
            [grid_rows[start : start + half], grid_rows[start + half : start + 2 * half]], axis=1
        ).astype(jnp.bfloat16)


def idft_call(table, received, lon_count, first, count):
    lat_count, held, _, wide = received.shape
    start = first // GROUP
    half = table.shape[0] // (2 * lon_count)
    return pl.pallas_call(
        functools.partial(idft_kernel, lon_count),
        grid=(count // GROUP, GROUP),
        in_specs=[
            pl.BlockSpec(table.shape, lambda g, t: (0, 0)),
            pl.BlockSpec((lat_count, held, GROUP, wide), lambda g, t: (0, 0, g + start, 0)),
        ],
        out_specs=[pl.BlockSpec((1, half, wide), lambda g, t: (g * GROUP + t, 0, 0))] * lon_count,
        out_shape=[jax.ShapeDtypeStruct((count, half, wide), jnp.bfloat16)] * lon_count,
        scratch_shapes=[wide_scratch(lat_count * held * GROUP, wide)],
        compiler_params=pltpu.CompilerParams(vmem_limit_bytes=VMEM_LIMIT),
        cost_estimate=cost(0.8 * count),
    )(table, received)


def legendre_kernel(spectral_count, forward, table_ref, gain_ref, quad_ref, *refs):
    ins = refs[:spectral_count]
    refs = refs[spectral_count:]
    table = table_ref[0]
    rows = jnp.concatenate([ref[:, 0].astype(jnp.float32) for ref in ins], axis=1)
    lat_total, wide = rows.shape[0] * rows.shape[1], rows.shape[2]
    spectral = rows.reshape(lat_total, wide).astype(jnp.bfloat16)
    coefs = jnp.dot(table, spectral, preferred_element_type=jnp.float32)
    if forward:
        cot_ref, outs, sum_ref = refs[0], refs[1:-1], refs[-1]

        @pl.when(pl.program_id(0) == 0)
        def _():
            sum_ref[...] = jnp.zeros_like(sum_ref)

        sum_ref[...] += coefs * cot_ref[0]
    else:
        outs = refs[:-1]
        refs[-1][0] = coefs
    filtered = (gain_ref[...] * coefs).astype(jnp.bfloat16)
    synth = lax.dot_general(
        table, filtered, (((0,), (0,)), ((), ())), preferred_element_type=jnp.float32
    )
    if not forward:
        synth = synth * quad_ref[...]
    synth = synth.reshape(rows.shape)
    start = 0
    for ref in outs:
        count = ref.shape[2]
        ref[:, 0] = synth[:, start : start + count].astype(jnp.bfloat16)
        start += count


def legendre_call(table, gain, quad_all, received, spans, cot_coefs):
    lat_count, held, _, wide = received[0].shape
    degrees, lat_total = table.shape[1:]
    forward = cot_coefs is not None

    def chunk_spec(count):
        return pl.BlockSpec((lat_count, 1, count, wide), lambda i: (0, i, 0, 0))

    coef_spec = pl.BlockSpec((1, degrees, wide), lambda i: (i, 0, 0))
    in_specs = [
        pl.BlockSpec((1, degrees, lat_total), lambda i: (i, 0, 0)),
        pl.BlockSpec(gain.shape, lambda i: (0, 0)),
        pl.BlockSpec(quad_all.shape, lambda i: (0, 0)),
    ] + [chunk_spec(chunk.shape[2]) for chunk in received]
    operands = [table, gain, quad_all] + list(received)
    out_specs = [chunk_spec(count) for _, count in spans]
    out_shape = [
        jax.ShapeDtypeStruct((lat_count, held, count, wide), jnp.bfloat16) for _, count in spans
    ]
    if forward:
        in_specs.append(coef_spec)
        operands.append(cot_coefs)
        out_specs.append(pl.BlockSpec((degrees, wide), lambda i: (0, 0)))
        out_shape.append(jax.ShapeDtypeStruct((degrees, wide), jnp.float32))
    else:
        out_specs.append(coef_spec)
        out_shape.append(jax.ShapeDtypeStruct((held, degrees, wide), jnp.float32))
    outs = pl.pallas_call(
        functools.partial(legendre_kernel, len(received), forward),
        grid=(held,),
        in_specs=in_specs,
        out_specs=out_specs,
        out_shape=out_shape,
        compiler_params=pltpu.CompilerParams(vmem_limit_bytes=VMEM_LIMIT),
        cost_estimate=cost(1.1 * held),
    )(*operands)
    return outs[:-1], outs[-1]


def cot_conv_kernel(lon_count, place_ref, conv_ref, cot_ref, *refs):
    pieces, out_ref, scratch = refs[:lon_count], refs[-2], refs[-1]
    cot_hidden = unpack_row([ref[0] for ref in pieces], place_ref[0], scratch)
    slope = gelu_slope(conv_ref[0].astype(jnp.float32))
    out_ref[0] = (cot_ref[0].astype(jnp.float32) + cot_hidden * slope).astype(jnp.bfloat16)


def result_kernel(lon_count, place_ref, conv_ref, *refs):
    pieces, out_ref, scratch = refs[:lon_count], refs[-2], refs[-1]
    branch = unpack_row([ref[0] for ref in pieces], place_ref[0], scratch)
    out_ref[0] = (conv_ref[0].astype(jnp.float32) + branch).astype(jnp.bfloat16)


def grid_call(kernel, place, conv_out, beside, pieces, first, count, held):
    lon_count = len(pieces)
    cols, chans = conv_out.shape[1:]
    half, wide = pieces[0].shape[1:]
    row_spec = pl.BlockSpec((1, cols, chans), lambda t: (t + first, 0, 0))
    piece_spec = pl.BlockSpec((1, half, wide), lambda t: (t, 0, 0))
    in_specs = [SMEM_SPEC, row_spec] + [row_spec] * len(beside) + [piece_spec] * lon_count
    operands = [place, conv_out] + beside + list(pieces)
    aliases = {}
    if held is not None:
        aliases = {len(operands): 0}
        in_specs.append(pl.BlockSpec(memory_space=pl.ANY))
        operands.append(held)
    return pl.pallas_call(
        functools.partial(kernel, lon_count),
        grid=(count,),
        in_specs=in_specs,
        out_specs=row_spec,
        out_shape=jax.ShapeDtypeStruct(conv_out.shape, jnp.bfloat16),
        scratch_shapes=[pltpu.VMEM((lon_count, half, wide), jnp.float32)],
        input_output_aliases=aliases,
        compiler_params=pltpu.CompilerParams(vmem_limit_bytes=VMEM_LIMIT),
        cost_estimate=cost(0.9 * count),
    )(*operands)


def edges(block, axis, dim, width, periodic):
    count = lax.axis_size(axis)
    forward = [(i, i + 1) for i in range(count - 1)]
    if periodic:
        forward.append((count - 1, 0))
    backward = [(target, source) for source, target in forward]
    size = block.shape[dim]
    low = lax.ppermute(lax.slice_in_dim(block, size - width, size, axis=dim), axis, forward)
    high = lax.ppermute(lax.slice_in_dim(block, 0, width, axis=dim), axis, backward)
    return low, high


def padded_field(field, lat_edges, *gates):
    low, high = lat_edges
    cols = field.shape[1]
    ends = jnp.concatenate(
        [jnp.concatenate([part[:, :DW], part[:, cols - DW :]], axis=1) for part in (low, field, high)],
        axis=0,
    )
    west, east = edges(ends, "lon", 1, DW, True)
    tall = jnp.concatenate([low, after(field, *gates), high], axis=0)
    west = jnp.pad(west, ((0, 0), (WEST - DW, 0), (0, 0)))
    east = jnp.pad(east, ((0, 0), (0, Q_BLOCK - P_BLOCK - WEST - DW), (0, 0)))
    return jnp.concatenate([west, tall, east], axis=1)


def after(value, *earlier):
    return lax.optimization_barrier((value,) + earlier)[0]


def swap(pieces, direction, earlier=None):
    count = lax.axis_size("lon")
    moved = [pieces[0]]
    for s in range(1, count):
        perm = [(i, (i + direction * s) % count) for i in range(count)]
        sent = pieces[s] if earlier is None else after(pieces[s], earlier)
        moved.append(lax.ppermute(sent, "lon", perm))
    return moved


def over_lat(blocks):
    return lax.all_to_all(blocks, "lat", split_axis=0, concat_axis=0, tiled=True)


def summed_everywhere(terms, gain_terms, gates, later_gate):
    lat_count, lon_count = lax.axis_size("lat"), lax.axis_size("lon")
    wide = terms.shape[1]
    parts = jnp.concatenate([terms, gain_terms], axis=1).astype(jnp.bfloat16)
    parts = parts.reshape(lat_count, -1, parts.shape[1])
    own = jnp.sum(over_lat(after(parts, *gates)).astype(jnp.float32), axis=0)
    pieces = jnp.stack(swap([own] * lon_count, 1))
    places = (lax.axis_index("lon") - jnp.arange(lon_count, dtype=jnp.int32)) % lon_count
    pieces = pieces[places]
    gains = [pieces[d, :, wide:] for d in range(lon_count)]
    total = jnp.concatenate([jnp.sum(pieces[:, :, :wide], axis=0)] + gains, axis=1).astype(jnp.bfloat16)
    shares = over_lat(after(jnp.broadcast_to(total[None], (lat_count,) + total.shape), later_gate))
    shares = shares.reshape(terms.shape[0], -1).astype(jnp.float32)
    return shares[:, :wide], shares[:, wide:]


def spans_of(*counts):
    spans, first = [], 0
    for count in counts:
        spans.append((first, count))
        first += count
    return spans


def body(
    source_field,
    cotangent,
    weight,
    spectral_gain,
    legendre,
    support_lat,
    support_lon,
    support_val,
    order_map,
):
    row_count, col_count, chan_count = source_field.shape
    lon_count, lat_count = lax.axis_size("lon"), lax.axis_size("lat")
    lat_total = row_count * lat_count
    band_index = lax.axis_index("lat")
    block_index = lax.axis_index("lon")
    share = chan_count // lon_count
    place = block_index.astype(jnp.int32).reshape(1)
    third = row_count // 3
    thirds = spans_of(third, third, row_count - 2 * third)
    spans = spans_of(row_count - third, third)

    back_places = (block_index - jnp.arange(lon_count, dtype=jnp.int32)) % lon_count
    longitude = (back_places[:, None] * col_count + jnp.arange(col_count, dtype=jnp.int32)).reshape(-1)
    orders = jnp.take(order_map.reshape(lat_count, lon_count, -1), back_places, axis=1).reshape(-1)
    inverse_table = dft_table(longitude, orders)
    forward_table = inverse_table.T
    all_rows = jnp.arange(lat_total, dtype=jnp.int32).astype(jnp.float32)
    quad_all = jnp.sin(math.pi * (all_rows + 0.5) / lat_total)
    quad_band = lax.dynamic_slice_in_dim(quad_all, band_index * row_count, row_count, 0)
    quad_rows = jnp.broadcast_to(quad_band[:, None, None], (row_count, 1, 2 * share))
    gain = lax.dynamic_slice_in_dim(spectral_gain, block_index * share, share, 1)
    gain = jnp.concatenate([gain, gain], axis=1)
    tap_weights = tap_table(support_lat, support_lon, support_val)
    tap_pad = jnp.pad(tap_weights, ((H, H), (0, 0), (0, 0), (0, 0)))
    tap_rows = lax.dynamic_slice_in_dim(tap_pad, band_index * row_count, row_count + 2 * H, 0)
    flat_weight = weight.reshape(K * chan_count, chan_count)
    flat_weight_back = weight.transpose(0, 2, 1).reshape(K * chan_count, chan_count)

    coefs = tap_coefficients(tap_rows, row_count, False)

    source_edges = edges(source_field, "lat", 0, H, False)
    packed = [pack_call(place, cotangent, lon_count, first, count) for first, count in thirds]
    padded_source, conv_out, hidden_pieces, last = None, None, [], None
    gates, cot_received, sent_gates = [pieces[0] for pieces in packed], [], source_edges
    for (first, count), pieces in zip(thirds, packed):
        lines = swap(pieces, 1, last)
        last = lines[-1]
        blocks = dft_call(
            forward_table, quad_rows, [[after(lines[0], *gates)] + lines[1:]], first, lat_count, False
        )
        cot_received.append(over_lat(after(blocks, *sent_gates)))
        sent_gates = [cot_received[-1]]
        if padded_source is None:
            padded_source = padded_field(source_field, source_edges, blocks)
        conv_out, pieces = conv_call(
            place, after(padded_source, blocks), coefs, flat_weight, col_count, lon_count, first, count, conv_out
        )
        gates = [conv_out]
        hidden_pieces.append(pieces)
    hidden_lines = []
    for pieces in hidden_pieces:
        hidden_lines.append(swap(pieces, 1, last))
        last = hidden_lines[-1][-1]
    table = jnp.concatenate(swap([legendre] * lon_count, 1, last), axis=0)
    hidden_received = []
    sent_gates.append(hidden_lines[1][-1])
    for first, lines in ((0, hidden_lines[:1]), (third, hidden_lines[1:])):
        if first == 0:
            lines = [[after(lines[0][0], conv_out)] + lines[0][1:]]
        blocks = dft_call(forward_table, quad_rows, lines, first, lat_count, True)
        hidden_received.append(over_lat(after(blocks, *sent_gates)))
        sent_gates = [hidden_received[-1]]

    quad_column = quad_all[:, None]
    cot_synth, cot_coefs = legendre_call(
        after(table, blocks), gain, quad_column, cot_received, thirds, None
    )
    outer_first = [0, 2, 1]
    first_back = over_lat(after(cot_synth[0], *sent_gates))
    synth, gain_terms = legendre_call(table, gain, quad_column, hidden_received, spans, cot_coefs)

    cot_conv, received, gates = None, first_back, [synth[0]]
    for step, index in enumerate(outer_first):
        first, count = thirds[index]
        later = synth[0] if step == 2 else cot_synth[outer_first[step + 1]]
        later = over_lat(after(later, received, *gates))
        pieces = idft_call(inverse_table, after(received, gates[0]), lon_count, 0, count)
        pieces = swap(pieces, -1, None if cot_conv is None else gates[0])
        cot_conv = grid_call(
            cot_conv_kernel, place, conv_out, [cotangent], pieces, first, count, cot_conv
        )
        received, gates = later, [pieces[-1]]
        if step == 1:
            cot_edges = edges(cot_conv, "lat", 0, H, False)
            gates += list(cot_edges)
    first_branch = received
    padded_cot = padded_field(cot_conv, cot_edges)
    coefs_back = tap_coefficients(tap_rows, row_count, True)
    (first, count), (last_first, last_count) = spans
    back = back_call(padded_cot, coefs_back, flat_weight_back, source_field, first, count, None)
    second_branch = over_lat(after(synth[1], first_branch, back[0]))
    lines = idft_call(inverse_table, after(first_branch, back[0]), lon_count, 0, count)
    grad_input, weight_part = back_call(
        after(padded_cot, lines[0]), coefs_back, flat_weight_back, source_field, last_first, last_count, back
    )
    first_lines = swap(lines, -1)
    second_lines = idft_call(inverse_table, after(second_branch, grad_input), lon_count, 0, spans[1][1])
    gates = [second_branch]
    second_lines = swap(second_lines, -1, first_lines[-1])
    result = None
    for (first, count), pieces in zip(spans, [first_lines, second_lines]):
        result = grid_call(result_kernel, place, conv_out, [], pieces, first, count, result)

    gain_part = gain_terms[:, :share] + gain_terms[:, share:]
    weight_total, gain_total = summed_everywhere(weight_part, gain_part, gates, second_lines[-1])
    weight_total = weight_total.reshape(chan_count, K, chan_count)
    grad_weight = weight_total.transpose(1, 0, 2) / math.sqrt(1.0 * lat_total * NLON)
    grad_gain = gain_total / math.sqrt(2.0 * M)
    return (result, grad_input, grad_weight, grad_gain)


def solution(mesh):
    return jax.shard_map(
        body,
        mesh=mesh,
        in_specs=(
            P("lat", "lon", None),
            P("lat", "lon", None),
            P(),
            P(),
            P(("lat", "lon"), None, None),
            P(),
            P(),
            P(),
            P(),
        ),
        out_specs=(P("lat", "lon", None), P("lat", "lon", None), P(), P()),
        check_vma=False,
    )
```
